32 devices in a mesh: groups: 2 (over y), row: 4 (over x, core), col: 4 (over z).
Axes of the slice: x: 2, y: 2, z: 4, core: 2. Of those that a mesh axis runs over, the one named last changes fastest.
Arguments:
- pair: bfloat16 [128, 64, 128], P(('groups', 'row'), 'col'), parts along dimension 0, may hold values from -6 to 6
- res_mask: int32 [128], P('groups'), parts along dimension 0, may hold values 0 or 1
- input_norm_gain: float32 [128], replicated, may hold values from 0.25 to 1.75
- input_norm_bias: float32 [128], replicated, may hold values from -3 to 3
- proj_left: bfloat16 [128, 256], replicated, may hold values from -0.5 to 0.5
- proj_right: bfloat16 [128, 256], replicated, may hold values from -0.5 to 0.5
- gate_out: bfloat16 [128, 128], replicated, may hold values from -0.5 to 0.5
- mid_gain: float32 [128], replicated, may hold values from 0.25 to 1.75
- mid_bias: float32 [128], replicated, may hold values from -3 to 3
- proj_out: bfloat16 [128, 128], replicated, may hold values from -0.5 to 0.5
- cotangent: bfloat16 [128, 64, 128], P(('groups', 'row'), 'col'), parts along dimension 0, may hold values from -6 to 6
Outputs:
- update: bfloat16 [128, 64, 128], P(('groups', 'row'), 'col'), parts along dimension 0
- pair_gradient: float32 [128, 64, 128], P(('groups', 'row'), 'col'), parts along dimension 0
- gain_gradient: float32 [256], P('groups'), parts along dimension 0
- grad_bias: float32 [256], P('groups'), parts along dimension 0
The draws below stay inside these ranges and needn't reach their ends.
There are 2 independent parts, one for each index of `groups`. The reference program is written for one: setup_inputs(seed, part) draws one part's arguments, and reference() takes and returns one part's arrays. A program takes and returns all parts, laid end to end along the dimension named above; an argument that names none is the same for every part. Nothing has to cross between parts.
Inputs may be any that keep to these rules, and one draw needn't show every extreme that they name: `res_mask`: 1 marks a present residue, 0 a padded one.
All inputs are finite; a program needn't handle non-finite values.
Results may differ from the reference program's by a relative error of at most 0.0074.
Values may be sent and summed in bfloat16 or wider, within the bound.
A program may use at most 64 MiB of HBM per device.

```python
import jax
import jax.numpy as jnp
from jax import lax

C = 128
CH = 128
RESIDUE_TOTAL = 64


def with_ends(array, rng, smallest, top_value):
    longest = array.shape.index(max(array.shape))
    spots = []
    for shift in (0, 1):
        where = [jax.random.randint(jax.random.fold_in(rng, axis), (), 0, length) for axis, length in enumerate(array.shape)]
        where[longest] = (where[longest] + shift) % array.shape[longest]
        spots.append(tuple(where))
    return array.at[spots[0]].set(smallest).at[spots[1]].set(top_value)


def block_levels(stream_key, dims, cuts, low, high):
    loudness = 1.0
    for axis_at, blocks in cuts:
        steps = jax.random.uniform(jax.random.fold_in(jax.random.fold_in(stream_key, 6), axis_at), (blocks,), jnp.float32, low / len(cuts), high / len(cuts))
        loudness = loudness * jnp.repeat(jnp.exp(steps), dims[axis_at] // blocks).reshape((-1,) + (1,) * (len(dims) - 1 - axis_at))
    return loudness


def bell_draw(rng, shape, scale, reach, pieces=(), kind=jnp.bfloat16):
    entries = jax.random.normal(rng, shape, jnp.float32) * scale
    if len(pieces) > 0:
        entries = block_levels(rng, shape, pieces, -0.22, 0.18) * entries
    return jnp.clip(entries, min=-reach, max=reach).astype(kind)


def setup_inputs(seed: int = 0, part: int = 0) -> dict:
    streams_of = jax.random.split(jax.random.key(seed), 12)
    own_keys = jax.random.split(jax.random.fold_in(streams_of[11], part), 12)
    return {
        "pair": bell_draw(own_keys[0], (RESIDUE_TOTAL, RESIDUE_TOTAL, C), 1.0, 6.0, ((0, 4), (1, 4))),
        "res_mask": with_ends((jax.random.randint(own_keys[1], (RESIDUE_TOTAL,), 0, 8) < 7).astype(jnp.int32), jax.random.fold_in(own_keys[1], 1), 0, 1),
        "input_norm_gain": jnp.clip(1.0 + 0.15 * jax.random.normal(streams_of[2], (C,), jnp.float32), 0.25, 1.75),
        "input_norm_bias": bell_draw(streams_of[3], (C,), 0.5, 3.0, (), jnp.float32),
        "proj_left": bell_draw(streams_of[4], (C, 2 * CH), C ** -0.5, 0.5),
        "proj_right": bell_draw(streams_of[5], (C, 2 * CH), C ** -0.5, 0.5),
        "gate_out": bell_draw(streams_of[6], (C, C), C ** -0.5, 0.5),
        "mid_gain": jnp.clip(1.0 + 0.15 * jax.random.normal(streams_of[7], (CH,), jnp.float32), 0.25, 1.75),
        "mid_bias": bell_draw(streams_of[8], (CH,), 0.5, 3.0, (), jnp.float32),
        "proj_out": bell_draw(streams_of[9], (CH, C), CH ** -0.5, 0.5),
        "cotangent": bell_draw(own_keys[10], (RESIDUE_TOTAL, RESIDUE_TOTAL, C), 1.0, 6.0, ((0, 4), (1, 4))),
    }


def apply_layer_norm(values):
    center = values - lax.optimization_barrier(jnp.mean(values, axis=-1, keepdims=True))
    reciprocal_deviation = lax.rsqrt(lax.optimization_barrier(jnp.mean(center * center, axis=-1, keepdims=True)) + 1e-05)
    return (center * reciprocal_deviation, reciprocal_deviation)

def layer_norm_backward(grad_hat, hatted, reciprocal_deviation):
    first = lax.optimization_barrier(jnp.mean(grad_hat, axis=-1, keepdims=True))
    second = lax.optimization_barrier(jnp.mean(grad_hat * hatted, axis=-1, keepdims=True))
    return (grad_hat - first - hatted * second) * reciprocal_deviation

def gating_back(grad_out, raw, pmask, width):
    sig = jax.nn.sigmoid(raw[..., :width])
    val = raw[..., width:]
    masked = grad_out * pmask
    return jnp.concatenate([masked * val * sig * (1.0 - sig), masked * sig], axis=-1).astype(jnp.bfloat16)

def reference(pair, res_mask, input_norm_gain, input_norm_bias, proj_left, proj_right, gate_out, mid_gain, mid_bias, proj_out, cotangent):
    standardized_input, reciprocal_deviation = apply_layer_norm(pair.astype(jnp.float32))
    normalized_pair = (standardized_input * input_norm_gain + input_norm_bias).astype(jnp.bfloat16)
    flat = normalized_pair.reshape(RESIDUE_TOTAL * RESIDUE_TOTAL, C)
    maskf = res_mask.astype(jnp.float32)
    pmask = (maskf[:, None] * maskf[None, :])[..., None]
    left = jnp.dot(flat, proj_left, preferred_element_type=jnp.float32).reshape(RESIDUE_TOTAL, RESIDUE_TOTAL, 2 * CH)
    right = jnp.dot(flat, proj_right, preferred_element_type=jnp.float32).reshape(RESIDUE_TOTAL, RESIDUE_TOTAL, 2 * CH)
    left_gated = (pmask * jax.nn.sigmoid(left[..., :CH]) * left[..., CH:]).astype(jnp.bfloat16)
    right_gated = (pmask * jax.nn.sigmoid(right[..., :CH]) * right[..., CH:]).astype(jnp.bfloat16)
    left32 = left_gated.astype(jnp.float32)
    right32 = right_gated.astype(jnp.float32)
    product = jnp.einsum('ikc,jkc->ijc', left32, right32, precision=lax.Precision.HIGHEST)
    ohat, oinv = apply_layer_norm(product)
    mid = (ohat * mid_gain + mid_bias).astype(jnp.bfloat16)
    value = jnp.dot(mid.reshape(RESIDUE_TOTAL * RESIDUE_TOTAL, CH), proj_out, preferred_element_type=jnp.float32).reshape(RESIDUE_TOTAL, RESIDUE_TOTAL, C)
    gate = jax.nn.sigmoid(jnp.dot(flat, gate_out, preferred_element_type=jnp.float32)).reshape(RESIDUE_TOTAL, RESIDUE_TOTAL, C)
    update = (gate * value).astype(jnp.bfloat16)
    upstream = cotangent.astype(jnp.float32)
    grad_value = (upstream * gate).astype(jnp.bfloat16)
    grad_gpre = (upstream * value * gate * (1.0 - gate)).astype(jnp.bfloat16)
    grad_mid = jnp.dot(grad_value.reshape(RESIDUE_TOTAL * RESIDUE_TOTAL, C), proj_out.T, preferred_element_type=jnp.float32).reshape(RESIDUE_TOTAL, RESIDUE_TOTAL, CH)
    grad_product = layer_norm_backward(grad_mid * mid_gain, ohat, oinv).astype(jnp.bfloat16)
    grad32 = grad_product.astype(jnp.float32)
    grad_lg = jnp.einsum('ijc,jkc->ikc', grad32, right32, precision=lax.Precision.HIGHEST)
    grad_rg = jnp.einsum('ijc,ikc->jkc', grad32, left32, precision=lax.Precision.HIGHEST)
    dleft = gating_back(grad_lg, left, pmask, CH).reshape(RESIDUE_TOTAL * RESIDUE_TOTAL, 2 * CH)
    dright = gating_back(grad_rg, right, pmask, CH).reshape(RESIDUE_TOTAL * RESIDUE_TOTAL, 2 * CH)
    normalized_gradient = jnp.dot(dleft, proj_left.T, preferred_element_type=jnp.float32)
    normalized_gradient = normalized_gradient + jnp.dot(dright, proj_right.T, preferred_element_type=jnp.float32)
    normalized_gradient = normalized_gradient + jnp.dot(grad_gpre.reshape(RESIDUE_TOTAL * RESIDUE_TOTAL, C), gate_out.T, preferred_element_type=jnp.float32)
    normalized_gradient = normalized_gradient.reshape(RESIDUE_TOTAL, RESIDUE_TOTAL, C)
    grad_bias = lax.optimization_barrier(jnp.sum(normalized_gradient, axis=(0, 1))) / RESIDUE_TOTAL
    gain_gradient = lax.optimization_barrier(jnp.sum(normalized_gradient * standardized_input, axis=(0, 1))) / RESIDUE_TOTAL
    pair_gradient = layer_norm_backward(normalized_gradient * input_norm_gain, standardized_input, reciprocal_deviation)
    return (update, pair_gradient, gain_gradient, grad_bias)
```

```python
import functools

import jax
import jax.numpy as jnp
from jax import lax
from jax.experimental import pallas as pl
from jax.experimental.pallas import tpu as pltpu
from jax.sharding import PartitionSpec as P

MESH = pl.DeviceIdType.MESH
F32 = jnp.float32
BF16 = jnp.bfloat16


def normalize(values):
    center = values - jnp.mean(values, axis=-1, keepdims=True)
    inverse = lax.rsqrt(jnp.mean(center * center, axis=-1, keepdims=True) + 1e-05)
    return center * inverse, inverse


def normalize_backward(grad_hat, hatted, inverse):
    first = jnp.mean(grad_hat, axis=-1, keepdims=True)
    second = jnp.mean(grad_hat * hatted, axis=-1, keepdims=True)
    return (grad_hat - first - hatted * second) * inverse


def dot(a, b):
    return jnp.dot(a, b, preferred_element_type=F32)


def dot_transposed(a, b):
    return lax.dot_general(a, b, (((1,), (1,)), ((), ())), preferred_element_type=F32)


def loop(low, high, body):
    if high - low <= 4:
        for step in range(low, high):
            body(step)
    else:
        lax.fori_loop(low, high, lambda step, _: (body(step), 0)[1], 0)


def kernel(
    side,
    pair_ref,
    mask_ref,
    gain_ref,
    bias_ref,
    pl_ref,
    pr_ref,
    go_ref,
    mgain_ref,
    mbias_ref,
    po_ref,
    cot_ref,
    update_ref,
    pgrad_ref,
    ggrad_ref,
    bgrad_ref,
    right_all,
    right32,
    left32,
    part_send,
    part_recv,
    grad_all,
    grad32,
    lg_sum,
    q_send,
    q_recv,
    stat_send,
    stat_recv,
    right_ssem,
    right_rsem,
    part_ssem,
    part_rsem,
    grad_ssem,
    grad_rsem,
    q_ssem,
    q_rsem,
    stat_ssem,
    stat_rsem,
):
    rows, cols, chans = pair_ref.shape
    pairs = rows * cols
    hidden = pl_ref.shape[1] // 2
    total = mask_ref.shape[1]
    peers = side * side
    row = lax.axis_index("row")
    col = lax.axis_index("col")
    me = row * side + col

    def device(r, c):
        return {"row": r, "col": c}

    barrier = pltpu.get_barrier_semaphore()

    def greet(step):
        other = me ^ step
        pl.semaphore_signal(
            barrier, inc=1, device_id=device(other // side, other % side), device_id_type=MESH
        )

    if peers <= 16:
        for step in range(1, peers):
            greet(step)
    else:
        lax.fori_loop(1, peers, lambda step, _: (greet(step), 0)[1], 0)

    xhat, inverse = normalize(pair_ref[...].reshape(pairs, chans).astype(F32))
    normed = (xhat * gain_ref[...] + bias_ref[...]).astype(BF16)

    spot = lax.broadcasted_iota(jnp.int32, (pairs, total), 0)
    lane = lax.broadcasted_iota(jnp.int32, (pairs, total), 1)
    maskf = mask_ref[...].astype(F32)
    mask_row = jnp.sum(
        jnp.where(lane == row * rows + spot // cols, maskf, 0.0), axis=-1, keepdims=True
    )
    mask_col = jnp.sum(
        jnp.where(lane == col * cols + spot % cols, maskf, 0.0), axis=-1, keepdims=True
    )
    pmask = mask_row * mask_col

    right = dot(normed, pr_ref[...])
    right_sig = jax.nn.sigmoid(right[:, :hidden])
    right_val = right[:, hidden:]
    right_all[row] = (pmask * right_sig * right_val).astype(BF16)

    pl.semaphore_wait(barrier, peers - 1)

    def right_copy(step):
        return pltpu.make_async_remote_copy(
            src_ref=right_all.at[row],
            dst_ref=right_all.at[row],
            send_sem=right_ssem.at[step],
            recv_sem=right_rsem.at[step],
            device_id=device(row ^ step, col),
            device_id_type=MESH,
        )

    loop(1, side, lambda step: right_copy(step).start())

    left = dot(normed, pl_ref[...])
    left_sig = jax.nn.sigmoid(left[:, :hidden])
    left_val = left[:, hidden:]
    left_gated = (pmask * left_sig * left_val).astype(BF16).astype(F32)
    left32[...] = left_gated.reshape(rows, cols, hidden)
    gate = jax.nn.sigmoid(dot(normed, go_ref[...]))

    def part_copy(slot, r, c, sem):
        return pltpu.make_async_remote_copy(
            src_ref=part_send.at[slot],
            dst_ref=part_recv.at[col],
            send_sem=part_ssem.at[sem],
            recv_sem=part_rsem.at[sem],
            device_id=device(r, c),
            device_id_type=MESH,
        )

    def product_block(step):
        block = row ^ step
        if not (isinstance(step, int) and step == 0):
            right_copy(step).wait_recv()
        base = pl.multiple_of(block * pairs, pairs)
        right32[pl.ds(base, pairs), :] = right_all[block].astype(F32)
        acc = None
        for k in range(cols):
            term = left32[:, k : k + 1, :] * right32[pl.ds(base + k, rows, stride=cols), :][None]
            acc = term if acc is None else acc + term
        part_send[block] = acc.reshape(pairs, hidden).astype(BF16)

        @pl.when(block != col)
        def _():
            part_copy(block, row, block, col ^ block).start()

    product_block(0)
    loop(1, side, product_block)

    held = [part_send[col].astype(F32)]

    if side <= 4:
        product = part_send[col].astype(F32)
        for step in range(1, side):
            part_copy(0, row, col ^ step, step).wait_recv()
            product = product + part_recv[col ^ step].astype(F32)
    else:

        def add_part(step, running):
            part_copy(0, row, col ^ step, step).wait_recv()
            return running + part_recv[col ^ step].astype(F32)

        product = lax.fori_loop(1, side, add_part, held[0])

    ohat, oinv = normalize(product)
    mid = (ohat * mgain_ref[...] + mbias_ref[...]).astype(BF16)
    value = dot(mid, po_ref[...])
    upstream = cot_ref[...].reshape(pairs, chans).astype(F32)
    grad_value = (upstream * gate).astype(BF16)
    grad_mid = dot_transposed(grad_value, po_ref[...])
    grad_product = normalize_backward(grad_mid * mgain_ref[...], ohat, oinv)
    grad_all[col] = grad_product.astype(BF16)

    def grad_copy(step):
        return pltpu.make_async_remote_copy(
            src_ref=grad_all.at[col],
            dst_ref=grad_all.at[col],
            send_sem=grad_ssem.at[step],
            recv_sem=grad_rsem.at[step],
            device_id=device(row, col ^ step),
            device_id_type=MESH,
        )

    loop(1, side, lambda step: grad_copy(step).start())

    update_ref[...] = (gate * value).astype(BF16).reshape(rows, cols, chans)
    grad_gpre = (upstream * value * gate * (1.0 - gate)).astype(BF16)

    def q_copy(slot, r, sem):
        return pltpu.make_async_remote_copy(
            src_ref=q_send.at[slot],
            dst_ref=q_recv.at[row],
            send_sem=q_ssem.at[sem],
            recv_sem=q_rsem.at[sem],
            device_id=device(r, col),
            device_id_type=MESH,
        )

    lg_sum[...] = jnp.zeros_like(lg_sum)

    def grad_block(step):
        block = col ^ step
        if not (isinstance(step, int) and step == 0):
            grad_copy(step).wait_recv()
        grad32[...] = grad_all[block].astype(F32).reshape(rows, cols, hidden)
        for j in range(cols):
            term = jnp.sum(grad32[:, j : j + 1, :] * left32[...], axis=0)
            q_send[block, j * cols : (j + 1) * cols, :] = term.astype(BF16)

        @pl.when(block != row)
        def _():
            q_copy(block, block, row ^ block).start()

        acc = lg_sum[...]
        base = pl.multiple_of(block * pairs, pairs)
        for j in range(cols):
            acc = acc + grad32[:, j : j + 1, :] * right32[pl.ds(base + j * cols, cols), :][None]
        lg_sum[...] = acc

    grad_block(0)
    loop(1, side, grad_block)

    def gating_back(grad_out, sig, val):
        masked = grad_out * pmask
        return jnp.concatenate([masked * val * sig * (1.0 - sig), masked * sig], axis=-1).astype(
            BF16
        )

    dleft = gating_back(lg_sum[...].reshape(pairs, hidden), left_sig, left_val)
    normalized_gradient = dot_transposed(dleft, pl_ref[...]) + dot_transposed(
        grad_gpre, go_ref[...]
    )

    def add_q(step, running):
        q_copy(0, row ^ step, step).wait_recv()
        return running + q_recv[row ^ step].astype(F32)

    grad_rg = q_send[row].astype(F32)
    if side <= 4:
        for step in range(1, side):
            grad_rg = add_q(step, grad_rg)
    else:
        grad_rg = lax.fori_loop(1, side, add_q, grad_rg)
    dright = gating_back(grad_rg, right_sig, right_val)
    normalized_gradient = normalized_gradient + dot_transposed(dright, pr_ref[...])

    stat_send[0:1, :] = jnp.sum(normalized_gradient, axis=0, keepdims=True)
    stat_send[1:2, :] = jnp.sum(normalized_gradient * xhat, axis=0, keepdims=True)

    def stat_copy(step):
        other = me ^ step
        return pltpu.make_async_remote_copy(
            src_ref=stat_send,
            dst_ref=stat_recv.at[step - 1],
            send_sem=stat_ssem,
            recv_sem=stat_rsem,
            device_id=device(other // side, other % side),
            device_id_type=MESH,
        )

    if peers <= 16:
        for step in range(1, peers):
            stat_copy(step).start()
    else:
        lax.fori_loop(1, peers, lambda step, _: (stat_copy(step).start(), 0)[1], 0)

    pgrad_ref[...] = normalize_backward(
        normalized_gradient * gain_ref[...], xhat, inverse
    ).reshape(rows, cols, chans)

    def sent(step):
        right_copy(step).wait_send()
        part_copy(0, row, col ^ step, step).wait_send()
        grad_copy(step).wait_send()
        q_copy(0, row ^ step, step).wait_send()

    loop(1, side, sent)
    pltpu.make_async_copy(stat_recv, stat_recv, stat_rsem).wait()
    stats = stat_send[...] + jnp.sum(stat_recv[...], axis=0)
    bgrad_ref[...] = stats[0:1, :] / total
    ggrad_ref[...] = stats[1:2, :] / total
    pltpu.make_async_copy(stat_recv, stat_recv, stat_ssem).wait()


def on_device(
    side,
    pair,
    res_mask,
    input_norm_gain,
    input_norm_bias,
    proj_left,
    proj_right,
    gate_out,
    mid_gain,
    mid_bias,
    proj_out,
    cotangent,
):
    rows, cols, chans = pair.shape
    hidden = proj_left.shape[1] // 2
    pairs = rows * cols
    blocks = (side, pairs, hidden)
    vmem = pl.BlockSpec(memory_space=pltpu.VMEM)
    update, pair_gradient, gain_gradient, grad_bias = pl.pallas_call(
        functools.partial(kernel, side),
        out_shape=(
            jax.ShapeDtypeStruct((rows, cols, chans), BF16),
            jax.ShapeDtypeStruct((rows, cols, chans), F32),
            jax.ShapeDtypeStruct((1, chans), F32),
            jax.ShapeDtypeStruct((1, chans), F32),
        ),
        in_specs=[vmem] * 11,
        out_specs=(vmem,) * 4,
        scratch_shapes=[
            pltpu.VMEM(blocks, BF16),
            pltpu.VMEM((side * pairs, hidden), F32),
            pltpu.VMEM((rows, cols, hidden), F32),
            pltpu.VMEM(blocks, BF16),
            pltpu.VMEM(blocks, BF16),
            pltpu.VMEM(blocks, BF16),
            pltpu.VMEM((rows, cols, hidden), F32),
            pltpu.VMEM((rows, cols, hidden), F32),
            pltpu.VMEM(blocks, BF16),
            pltpu.VMEM(blocks, BF16),
            pltpu.VMEM((2, chans), F32),
            pltpu.VMEM((side * side - 1, 2, chans), F32),
        ]
        + [pltpu.SemaphoreType.DMA((side,))] * 8
        + [pltpu.SemaphoreType.DMA] * 2,
        compiler_params=pltpu.CompilerParams(
            collective_id=0, has_side_effects=True, vmem_limit_bytes=40 * 1024 * 1024
        ),
        name="triangle",
    )(
        pair,
        res_mask.reshape(1, -1),
        input_norm_gain.reshape(1, -1),
        input_norm_bias.reshape(1, -1),
        proj_left,
        proj_right,
        gate_out,
        mid_gain.reshape(1, -1),
        mid_bias.reshape(1, -1),
        proj_out,
        cotangent,
    )
    return update, pair_gradient, gain_gradient.reshape(-1), grad_bias.reshape(-1)


def solution(mesh):
    blocks = P(("groups", "row"), "col", None)
    return jax.shard_map(
        functools.partial(on_device, mesh.shape["row"]),
        mesh=mesh,
        in_specs=(blocks, P("groups")) + (P(),) * 8 + (blocks,),
        out_specs=(blocks, blocks, P("groups"), P("groups")),
        check_vma=False,
    )
```

```python
import functools

import jax
import jax.numpy as jnp
from jax import lax
from jax.experimental import pallas as pl
from jax.experimental.pallas import tpu as pltpu
from jax.sharding import PartitionSpec as P

MESH = pl.DeviceIdType.MESH
F32 = jnp.float32
BF16 = jnp.bfloat16
VMEM_LIMIT = 62 * 1024 * 1024
HALVES = 2


def normalize(values):
    center = values - jnp.mean(values, axis=-1, keepdims=True)
    inverse = lax.rsqrt(jnp.mean(center * center, axis=-1, keepdims=True) + 1e-05)
    return center * inverse, inverse


def normalize_backward(grad_hat, hatted, inverse):
    first = jnp.mean(grad_hat, axis=-1, keepdims=True)
    second = jnp.mean(grad_hat * hatted, axis=-1, keepdims=True)
    return (grad_hat - first - hatted * second) * inverse


def dot(a, b):
    return jnp.dot(a, b, preferred_element_type=F32)


def dot_transposed(a, b):
    return lax.dot_general(a, b, (((1,), (1,)), ((), ())), preferred_element_type=F32)


def loop(low, high, body):
    if high - low <= 4:
        for step in range(low, high):
            body(step)
    else:
        lax.fori_loop(low, high, lambda step, _: (body(step), 0)[1], 0)


def kernel(
    side,
    pair_hbm,
    mask_hbm,
    gain_hbm,
    bias_hbm,
    pl_hbm,
    pr_hbm,
    go_hbm,
    mgain_hbm,
    mbias_hbm,
    po_hbm,
    cot_hbm,
    update_hbm,
    pgrad_hbm,
    stats_hbm,
    update_ref,
    pgrad_ref,
    stats_ref,
    pair_ref,
    mask_ref,
    gain_ref,
    bias_ref,
    pl_ref,
    pr_ref,
    go_ref,
    mgain_ref,
    mbias_ref,
    po_ref,
    cot_ref,
    load_sem,
    store_sem,
    right_all,
    right32,
    left32,
    part_send,
    part_recv,
    grad_all,
    grad32,
    lg_sum,
    q_sum,
    q_send,
    q_recv,
    stat_send,
    stat_recv,
    right_ssem,
    right_rsem,
    part_ssem,
    part_rsem,
    grad_ssem,
    grad_rsem,
    q_ssem,
    q_rsem,
    stat_ssem,
    stat_rsem,
):
    loads = [
        pltpu.make_async_copy(source, target, load_sem.at[index])
        for index, (source, target) in enumerate(
            (
                (pair_hbm, pair_ref),
                (gain_hbm, gain_ref),
                (bias_hbm, bias_ref),
                (mask_hbm, mask_ref),
                (pr_hbm, pr_ref),
                (pl_hbm, pl_ref),
                (go_hbm, go_ref),
                (cot_hbm, cot_ref),
                (po_hbm, po_ref),
                (mgain_hbm, mgain_ref),
                (mbias_hbm, mbias_ref),
            )
        )
    ]
    for load in loads:
        load.start()

    rows, cols, chans = pair_ref.shape
    pairs = rows * cols
    hidden = pl_ref.shape[1] // 2
    total = mask_ref.shape[1]
    peers = side * side
    row = lax.axis_index("row")
    col = lax.axis_index("col")
    me = row * side + col

    def device(r, c):
        return {"row": r, "col": c}

    barrier = pltpu.get_barrier_semaphore()

    def greet(step):
        other = me ^ step
        pl.semaphore_signal(
            barrier, inc=1, device_id=device(other // side, other % side), device_id_type=MESH
        )

    if peers <= 16:
        for step in range(1, peers):
            greet(step)
    else:
        lax.fori_loop(1, peers, lambda step, _: (greet(step), 0)[1], 0)

    loads[0].wait()
    xhat, inverse = normalize(pair_ref[...].reshape(pairs, chans).astype(F32))
    for load in loads[1:5]:
        load.wait()
    normed = (xhat * gain_ref[...] + bias_ref[...]).astype(BF16)

    spot = lax.broadcasted_iota(jnp.int32, (pairs, total), 0)
    lane = lax.broadcasted_iota(jnp.int32, (pairs, total), 1)
    maskf = mask_ref[...].astype(F32)
    mask_row = jnp.sum(
        jnp.where(lane == row * rows + spot // cols, maskf, 0.0), axis=-1, keepdims=True
    )
    mask_col = jnp.sum(
        jnp.where(lane == col * cols + spot % cols, maskf, 0.0), axis=-1, keepdims=True
    )
    pmask = mask_row * mask_col

    right = dot(normed, pr_ref[...])
    right_sig = jax.nn.sigmoid(right[:, :hidden])
    right_val = right[:, hidden:]
    right_all[row] = (pmask * right_sig * right_val).astype(BF16)

    pl.semaphore_wait(barrier, peers - 1)

    def right_copy(step):
        return pltpu.make_async_remote_copy(
            src_ref=right_all.at[row],
            dst_ref=right_all.at[row],
            send_sem=right_ssem.at[step],
            recv_sem=right_rsem.at[step],
            device_id=device(row ^ step, col),
            device_id_type=MESH,
        )

    loop(1, side, lambda step: right_copy(step).start())

    for load in loads[5:]:
        load.wait()
    left = dot(normed, pl_ref[...])
    left_sig = jax.nn.sigmoid(left[:, :hidden])
    left_val = left[:, hidden:]
    left_gated = (pmask * left_sig * left_val).astype(BF16).astype(F32)
    left32[...] = left_gated.reshape(rows, cols, hidden)
    gate = jax.nn.sigmoid(dot(normed, go_ref[...]))

    part = pairs // HALVES
    span = rows // HALVES

    def part_copy(half, slot, c, step):
        place = pl.ds(half * part, part)
        return pltpu.make_async_remote_copy(
            src_ref=part_send.at[slot, place],
            dst_ref=part_recv.at[col, place],
            send_sem=part_ssem.at[half, step],
            recv_sem=part_rsem.at[half, step],
            device_id=device(row, c),
            device_id_type=MESH,
        )

    def take_right(step):
        block = row ^ step
        if not (isinstance(step, int) and step == 0):
            right_copy(step).wait_recv()
        base = pl.multiple_of(block * pairs, pairs)
        right32[pl.ds(base, pairs), :] = right_all[block].astype(F32)

    def product_block(half, step):
        block = row ^ step
        base = pl.multiple_of(block * pairs, pairs)
        acc = None
        for k in range(cols):
            term = (
                left32[half * span : (half + 1) * span, k : k + 1, :]
                * right32[pl.ds(base + k, rows, stride=cols), :][None]
            )
            acc = term if acc is None else acc + term
        part_send[block, half * part : (half + 1) * part, :] = acc.reshape(part, hidden).astype(
            BF16
        )

        @pl.when(block != col)
        def _():
            part_copy(half, block, block, col ^ block).start()

    take_right(0)
    for half in range(HALVES):
        product_block(half, 0)
    if side <= 4:
        for step in range(1, side // 2):
            take_right(step)
            for half in range(HALVES):
                product_block(half, step)
        for step in range(side // 2, side):
            take_right(step)
            product_block(0, step)
        for half in range(1, HALVES):
            for step in range(side // 2, side):
                product_block(half, step)
    else:

        def take_and_multiply(step):
            take_right(step)
            for half in range(HALVES):
                product_block(half, step)

        loop(1, side, take_and_multiply)

    def grad_copy(half, step):
        place = pl.ds(half * part, part)
        return pltpu.make_async_remote_copy(
            src_ref=grad_all.at[col, place],
            dst_ref=grad_all.at[col, place],
            send_sem=grad_ssem.at[half, step],
            recv_sem=grad_rsem.at[half, step],
            device_id=device(row, col ^ step),
            device_id_type=MESH,
        )

    upstream = cot_ref[...].reshape(pairs, chans).astype(F32)
    grad_value = (upstream * gate).astype(BF16)
    grad_mid = dot_transposed(grad_value, po_ref[...]) * mgain_ref[...]
    values = []

    for half in range(HALVES):
        own = slice(half * part, (half + 1) * part)

        def add_part(step, running):
            part_copy(half, 0, col ^ step, step).wait_recv()
            return running + part_recv[col ^ step, own, :].astype(F32)

        product = part_send[col, own, :].astype(F32)
        if side <= 4:
            for step in range(1, side):
                product = add_part(step, product)
        else:
            product = lax.fori_loop(1, side, add_part, product)
        ohat, oinv = normalize(product)
        grad_product = normalize_backward(grad_mid[own], ohat, oinv)
        grad_all[col, own, :] = grad_product.astype(BF16)
        loop(1, side, lambda step: grad_copy(half, step).start())
        mid = (ohat * mgain_ref[...] + mbias_ref[...]).astype(BF16)
        values.append(dot(mid, po_ref[...]))

    value = jnp.concatenate(values, axis=0)
    update_ref[...] = (gate * value).astype(BF16).reshape(rows, cols, chans)
    update_store = pltpu.make_async_copy(update_ref, update_hbm, store_sem.at[0])
    update_store.start()
    grad_gpre = (upstream * value * gate * (1.0 - gate)).astype(BF16)

    def q_copy(slot, r, sem):
        return pltpu.make_async_remote_copy(
            src_ref=q_send.at[slot],
            dst_ref=q_recv.at[row],
            send_sem=q_ssem.at[sem],
            recv_sem=q_rsem.at[sem],
            device_id=device(r, col),
            device_id_type=MESH,
        )

    lg_sum[...] = jnp.zeros_like(lg_sum)

    def grad_block(half, step):
        block = col ^ step
        own = slice(half * part, (half + 1) * part)
        mine = slice(half * span, (half + 1) * span)
        if not (isinstance(step, int) and step == 0):
            grad_copy(half, step).wait_recv()
        grad32[...] = grad_all[block, own, :].astype(F32).reshape(span, cols, hidden)
        for j in range(cols):
            term = jnp.sum(grad32[:, j : j + 1, :] * left32[mine], axis=0)
            where = slice(j * cols, (j + 1) * cols)
            if half > 0:
                term = term + q_sum[block, where, :]
            if half < HALVES - 1:
                q_sum[block, where, :] = term
            else:
                q_send[block, where, :] = term.astype(BF16)

        if half == HALVES - 1:

            @pl.when(block != row)
            def _():
                q_copy(block, block, row ^ block).start()

        acc = lg_sum[mine]
        base = pl.multiple_of(block * pairs, pairs)
        for j in range(cols):
            acc = acc + grad32[:, j : j + 1, :] * right32[pl.ds(base + j * cols, cols), :][None]
        lg_sum[mine] = acc

    for half in range(HALVES):
        grad_block(half, 0)
        loop(1, side, functools.partial(grad_block, half))

    def gating_back(grad_out, sig, val):
        masked = grad_out * pmask
        return jnp.concatenate([masked * val * sig * (1.0 - sig), masked * sig], axis=-1).astype(
            BF16
        )

    dleft = gating_back(lg_sum[...].reshape(pairs, hidden), left_sig, left_val)
    normalized_gradient = dot_transposed(dleft, pl_ref[...]) + dot_transposed(
        grad_gpre, go_ref[...]
    )

    def add_q(step, running):
        q_copy(0, row ^ step, step).wait_recv()
        return running + q_recv[row ^ step].astype(F32)

    grad_rg = q_send[row].astype(F32)
    if side <= 4:
        for step in range(1, side):
            grad_rg = add_q(step, grad_rg)
    else:
        grad_rg = lax.fori_loop(1, side, add_q, grad_rg)
    dright = gating_back(grad_rg, right_sig, right_val)
    normalized_gradient = normalized_gradient + dot_transposed(dright, pr_ref[...])

    stat_send[0:1, :] = jnp.sum(normalized_gradient, axis=0, keepdims=True)
    stat_send[1:2, :] = jnp.sum(normalized_gradient * xhat, axis=0, keepdims=True)

    def stat_copy(step):
        other = me ^ step
        return pltpu.make_async_remote_copy(
            src_ref=stat_send,
            dst_ref=stat_recv.at[step - 1],
            send_sem=stat_ssem,
            recv_sem=stat_rsem,
            device_id=device(other // side, other % side),
            device_id_type=MESH,
        )

    if peers <= 16:
        for step in range(1, peers):
            stat_copy(step).start()
    else:
        lax.fori_loop(1, peers, lambda step, _: (stat_copy(step).start(), 0)[1], 0)

    pgrad_ref[...] = normalize_backward(
        normalized_gradient * gain_ref[...], xhat, inverse
    ).reshape(rows, cols, chans)
    pgrad_store = pltpu.make_async_copy(pgrad_ref, pgrad_hbm, store_sem.at[1])
    pgrad_store.start()

    def sent(step):
        right_copy(step).wait_send()
        for half in range(HALVES):
            part_copy(half, 0, col ^ step, step).wait_send()
            grad_copy(half, step).wait_send()
        q_copy(0, row ^ step, step).wait_send()

    loop(1, side, sent)
    pltpu.make_async_copy(stat_recv, stat_recv, stat_rsem).wait()
    stats = stat_send[...] + jnp.sum(stat_recv[...], axis=0)
    stats_ref[...] = stats / total
    stats_store = pltpu.make_async_copy(stats_ref, stats_hbm, store_sem.at[2])
    stats_store.start()
    pltpu.make_async_copy(stat_recv, stat_recv, stat_ssem).wait()
    update_store.wait()
    pgrad_store.wait()
    stats_store.wait()


def finish(update_ref, pgrad_ref, stats_ref, update_hbm, pgrad_hbm, ggrad_hbm, bgrad_hbm, sem):
    copies = [
        pltpu.make_async_copy(source, target, sem.at[index])
        for index, (source, target) in enumerate(
            (
                (pgrad_ref, pgrad_hbm),
                (update_ref, update_hbm),
                (stats_ref.at[1:2], ggrad_hbm),
                (stats_ref.at[0:1], bgrad_hbm),
            )
        )
    ]
    for copy in copies:
        copy.start()
    for copy in copies:
        copy.wait()


def on_device(
    side,
    pair,
    res_mask,
    input_norm_gain,
    input_norm_bias,
    proj_left,
    proj_right,
    gate_out,
    mid_gain,
    mid_bias,
    proj_out,
    cotangent,
):
    rows, cols, chans = pair.shape
    hidden = proj_left.shape[1] // 2
    pairs = rows * cols
    blocks = (side, pairs, hidden)
    hbm = pl.BlockSpec(memory_space=pltpu.HBM)
    block = (rows, cols, chans)
    update, pair_gradient, stats = pl.pallas_call(
        functools.partial(kernel, side),
        out_shape=(
            jax.ShapeDtypeStruct((rows, cols, chans), BF16),
            jax.ShapeDtypeStruct((rows, cols, chans), F32),
            jax.ShapeDtypeStruct((2, chans), F32),
        ),
        in_specs=[hbm] * 11,
        out_specs=(hbm,) * 3,
        scratch_shapes=[
            pltpu.VMEM(block, BF16),
            pltpu.VMEM(block, F32),
            pltpu.VMEM((2, chans), F32),
            pltpu.VMEM(block, BF16),
            pltpu.VMEM((1, res_mask.shape[0]), jnp.int32),
            pltpu.VMEM((1, chans), F32),
            pltpu.VMEM((1, chans), F32),
            pltpu.VMEM(proj_left.shape, BF16),
            pltpu.VMEM(proj_right.shape, BF16),
            pltpu.VMEM(gate_out.shape, BF16),
            pltpu.VMEM((1, hidden), F32),
            pltpu.VMEM((1, hidden), F32),
            pltpu.VMEM(proj_out.shape, BF16),
            pltpu.VMEM(block, BF16),
            pltpu.SemaphoreType.DMA((11,)),
            pltpu.SemaphoreType.DMA((3,)),
            pltpu.VMEM(blocks, BF16),
            pltpu.VMEM((side * pairs, hidden), F32),
            pltpu.VMEM((rows, cols, hidden), F32),
            pltpu.VMEM(blocks, BF16),
            pltpu.VMEM(blocks, BF16),
            pltpu.VMEM(blocks, BF16),
            pltpu.VMEM((rows // HALVES, cols, hidden), F32),
            pltpu.VMEM((rows, cols, hidden), F32),
            pltpu.VMEM(blocks, F32),
            pltpu.VMEM(blocks, BF16),
            pltpu.VMEM(blocks, BF16),
            pltpu.VMEM((2, chans), F32),
            pltpu.VMEM((side * side - 1, 2, chans), F32),
        ]
        + [pltpu.SemaphoreType.DMA((side,))] * 2
        + [pltpu.SemaphoreType.DMA((HALVES, side))] * 4
        + [pltpu.SemaphoreType.DMA((side,))] * 2
        + [pltpu.SemaphoreType.DMA] * 2,
        compiler_params=pltpu.CompilerParams(
            collective_id=0, has_side_effects=True, vmem_limit_bytes=VMEM_LIMIT
        ),
        name="triangle",
    )(
        pair,
        res_mask.reshape(1, -1),
        input_norm_gain.reshape(1, -1),
        input_norm_bias.reshape(1, -1),
        proj_left,
        proj_right,
        gate_out,
        mid_gain.reshape(1, -1),
        mid_bias.reshape(1, -1),
        proj_out,
        cotangent,
    )
    update, pair_gradient, gain_gradient, grad_bias = pl.pallas_call(
        finish,
        out_shape=(
            jax.ShapeDtypeStruct(block, BF16),
            jax.ShapeDtypeStruct(block, F32),
            jax.ShapeDtypeStruct((1, chans), F32),
            jax.ShapeDtypeStruct((1, chans), F32),
        ),
        in_specs=[hbm] * 3,
        out_specs=(hbm,) * 4,
        scratch_shapes=[pltpu.SemaphoreType.DMA((4,))],
        compiler_params=pltpu.CompilerParams(vmem_limit_bytes=VMEM_LIMIT),
        name="finish",
    )(update, pair_gradient, stats)
    return update, pair_gradient, gain_gradient.reshape(-1), grad_bias.reshape(-1)


def solution(mesh):
    blocks = P(("groups", "row"), "col", None)
    return jax.shard_map(
        functools.partial(on_device, mesh.shape["row"]),
        mesh=mesh,
        in_specs=(blocks, P("groups")) + (P(),) * 8 + (blocks,),
        out_specs=(blocks, blocks, P("groups"), P("groups")),
        check_vma=False,
    )
```

```python
import functools

import jax
import jax.numpy as jnp
from jax import lax
from jax.experimental import pallas as pl
from jax.experimental.pallas import tpu as pltpu
from jax.sharding import PartitionSpec as P

MESH = pl.DeviceIdType.MESH
F32 = jnp.float32
BF16 = jnp.bfloat16
VMEM_LIMIT = 62 * 1024 * 1024
HALVES = 2


def normalize(values):
    center = values - jnp.mean(values, axis=-1, keepdims=True)
    inverse = lax.rsqrt(jnp.mean(center * center, axis=-1, keepdims=True) + 1e-05)
    return center * inverse, inverse


def normalize_backward(grad_hat, hatted, inverse):
    first = jnp.mean(grad_hat, axis=-1, keepdims=True)
    second = jnp.mean(grad_hat * hatted, axis=-1, keepdims=True)
    return (grad_hat - first - hatted * second) * inverse


def dot(a, b):
    return jnp.dot(a, b, preferred_element_type=F32)


def dot_transposed(a, b):
    return lax.dot_general(a, b, (((1,), (1,)), ((), ())), preferred_element_type=F32)


def loop(low, high, body):
    if high - low <= 4:
        for step in range(low, high):
            body(step)
    else:
        lax.fori_loop(low, high, lambda step, _: (body(step), 0)[1], 0)


def kernel(
    side,
    pair_hbm,
    mask_hbm,
    gain_hbm,
    bias_hbm,
    pl_hbm,
    pr_hbm,
    go_hbm,
    mgain_hbm,
    mbias_hbm,
    po_hbm,
    cot_hbm,
    update_hbm,
    pgrad_hbm,
    stats_hbm,
    update_ref,
    pgrad_ref,
    stats_ref,
    pair_ref,
    mask_ref,
    gain_ref,
    bias_ref,
    pl_ref,
    pr_ref,
    go_ref,
    mgain_ref,
    mbias_ref,
    po_ref,
    cot_ref,
    load_sem,
    store_sem,
    right_all,
    right32,
    left32,
    part_send,
    part_recv,
    grad_all,
    grad32,
    lg_sum,
    q_sum,
    q_send,
    q_recv,
    stat_send,
    stat_recv,
    right_ssem,
    right_rsem,
    part_ssem,
    part_rsem,
    grad_ssem,
    grad_rsem,
    q_ssem,
    q_rsem,
    stat_ssem,
    stat_rsem,
):
    loads = [
        pltpu.make_async_copy(source, target, load_sem.at[index])
        for index, (source, target) in enumerate(
            (
                (pair_hbm, pair_ref),
                (gain_hbm, gain_ref),
                (bias_hbm, bias_ref),
                (mask_hbm, mask_ref),
                (pr_hbm, pr_ref),
                (pl_hbm, pl_ref),
                (go_hbm, go_ref),
                (cot_hbm, cot_ref),
                (po_hbm, po_ref),
                (mgain_hbm, mgain_ref),
                (mbias_hbm, mbias_ref),
            )
        )
    ]
    for load in loads:
        load.start()

    rows, cols, chans = pair_ref.shape
    pairs = rows * cols
    hidden = pl_ref.shape[1] // 2
    total = mask_ref.shape[1]
    peers = side * side
    row = lax.axis_index("row")
    col = lax.axis_index("col")
    me = row * side + col

    def device(r, c):
        return {"row": r, "col": c}

    barrier = pltpu.get_barrier_semaphore()

    def greet(step):
        other = me ^ step
        pl.semaphore_signal(
            barrier, inc=1, device_id=device(other // side, other % side), device_id_type=MESH
        )

    if peers <= 16:
        for step in range(1, peers):
            greet(step)
    else:
        lax.fori_loop(1, peers, lambda step, _: (greet(step), 0)[1], 0)

    loads[0].wait()
    xhat, inverse = normalize(pair_ref[...].reshape(pairs, chans).astype(F32))
    for load in loads[1:5]:
        load.wait()
    normed = (xhat * gain_ref[...] + bias_ref[...]).astype(BF16)

    spot = lax.broadcasted_iota(jnp.int32, (pairs, total), 0)
    lane = lax.broadcasted_iota(jnp.int32, (pairs, total), 1)
    maskf = mask_ref[...].astype(F32)
    mask_row = jnp.sum(
        jnp.where(lane == row * rows + spot // cols, maskf, 0.0), axis=-1, keepdims=True
    )
    mask_col = jnp.sum(
        jnp.where(lane == col * cols + spot % cols, maskf, 0.0), axis=-1, keepdims=True
    )
    pmask = mask_row * mask_col

    right = dot(normed, pr_ref[...])
    right_sig = jax.nn.sigmoid(right[:, :hidden])
    right_val = right[:, hidden:]
    right_all[row] = (pmask * right_sig * right_val).astype(BF16)

    pl.semaphore_wait(barrier, peers - 1)

    def right_copy(step):
        return pltpu.make_async_remote_copy(
            src_ref=right_all.at[row],
            dst_ref=right_all.at[row],
            send_sem=right_ssem.at[step],
            recv_sem=right_rsem.at[step],
            device_id=device(row ^ step, col),
            device_id_type=MESH,
        )

    loop(1, side, lambda step: right_copy(step).start())

    for load in loads[5:]:
        load.wait()
    left = dot(normed, pl_ref[...])
    left_sig = jax.nn.sigmoid(left[:, :hidden])
    left_val = left[:, hidden:]
    left_gated = (pmask * left_sig * left_val).astype(BF16).astype(F32)
    left32[...] = left_gated.reshape(rows, cols, hidden)
    gate = jax.nn.sigmoid(dot(normed, go_ref[...]))

    part = pairs // HALVES
    span = rows // HALVES

    def part_copy(half, slot, c, step):
        place = pl.ds(half * part, part)
        return pltpu.make_async_remote_copy(
            src_ref=part_send.at[slot, place],
            dst_ref=part_recv.at[col, place],
            send_sem=part_ssem.at[half, step],
            recv_sem=part_rsem.at[half, step],
            device_id=device(row, c),
            device_id_type=MESH,
        )

    def take_right(step):
        block = row ^ step
        if not (isinstance(step, int) and step == 0):
            right_copy(step).wait_recv()
        base = pl.multiple_of(block * pairs, pairs)
        right32[pl.ds(base, pairs), :] = right_all[block].astype(F32)

    def product_block(half, step):
        block = row ^ step
        base = pl.multiple_of(block * pairs, pairs)
        acc = None
        for k in range(cols):
            term = (
                left32[half * span : (half + 1) * span, k : k + 1, :]
                * right32[pl.ds(base + k, rows, stride=cols), :][None]
            )
            acc = term if acc is None else acc + term
        part_send[block, half * part : (half + 1) * part, :] = acc.reshape(part, hidden).astype(
            BF16
        )

        @pl.when(block != col)
        def _():
            part_copy(half, block, block, col ^ block).start()

    take_right(0)
    for half in range(HALVES):
        product_block(half, 0)
    if side <= 4:
        for step in range(1, side // 2):
            take_right(step)
            for half in range(HALVES):
                product_block(half, step)
        for step in range(side // 2, side):
            take_right(step)
            product_block(0, step)
        for half in range(1, HALVES):
            for step in range(side // 2, side):
                product_block(half, step)
    else:

        def take_and_multiply(step):
            take_right(step)
            for half in range(HALVES):
                product_block(half, step)

        loop(1, side, take_and_multiply)

    def grad_copy(half, step):
        place = pl.ds(half * part, part)
        return pltpu.make_async_remote_copy(
            src_ref=grad_all.at[col, place],
            dst_ref=grad_all.at[col, place],
            send_sem=grad_ssem.at[half, step],
            recv_sem=grad_rsem.at[half, step],
            device_id=device(row, col ^ step),
            device_id_type=MESH,
        )

    upstream = cot_ref[...].reshape(pairs, chans).astype(F32)
    grad_value = (upstream * gate).astype(BF16)
    grad_mid = dot_transposed(grad_value, po_ref[...]) * mgain_ref[...]
    values = []

    for half in range(HALVES):
        own = slice(half * part, (half + 1) * part)

        def add_part(step, running):
            part_copy(half, 0, col ^ step, step).wait_recv()
            return running + part_recv[col ^ step, own, :].astype(F32)

        product = part_send[col, own, :].astype(F32)
        if side <= 4:
            for step in range(1, side):
                product = add_part(step, product)
        else:
            product = lax.fori_loop(1, side, add_part, product)
        ohat, oinv = normalize(product)
        grad_product = normalize_backward(grad_mid[own], ohat, oinv)
        grad_all[col, own, :] = grad_product.astype(BF16)
        loop(1, side, lambda step: grad_copy(half, step).start())
        mid = (ohat * mgain_ref[...] + mbias_ref[...]).astype(BF16)
        values.append(dot(mid, po_ref[...]))

    value = jnp.concatenate(values, axis=0)
    update_ref[...] = (gate * value).astype(BF16).reshape(rows, cols, chans)
    update_store = pltpu.make_async_copy(update_ref, update_hbm, store_sem.at[0])
    update_store.start()
    grad_gpre = (upstream * value * gate * (1.0 - gate)).astype(BF16)

    def q_copy(slot, r, sem):
        return pltpu.make_async_remote_copy(
            src_ref=q_send.at[slot],
            dst_ref=q_recv.at[row],
            send_sem=q_ssem.at[sem],
            recv_sem=q_rsem.at[sem],
            device_id=device(r, col),
            device_id_type=MESH,
        )

    lg_sum[...] = jnp.zeros_like(lg_sum)

    def grad_block(half, step):
        block = col ^ step
        own = slice(half * part, (half + 1) * part)
        mine = slice(half * span, (half + 1) * span)
        if not (isinstance(step, int) and step == 0):
            grad_copy(half, step).wait_recv()
        grad32[...] = grad_all[block, own, :].astype(F32).reshape(span, cols, hidden)
        for j in range(cols):
            term = jnp.sum(grad32[:, j : j + 1, :] * left32[mine], axis=0)
            where = slice(j * cols, (j + 1) * cols)
            if half > 0:
                term = term + q_sum[block, where, :]
            if half < HALVES - 1:
                q_sum[block, where, :] = term
            else:
                q_send[block, where, :] = term.astype(BF16)

        if half == HALVES - 1:

            @pl.when(block != row)
            def _():
                q_copy(block, block, row ^ block).start()

        acc = lg_sum[mine]
        base = pl.multiple_of(block * pairs, pairs)
        for j in range(cols):
            acc = acc + grad32[:, j : j + 1, :] * right32[pl.ds(base + j * cols, cols), :][None]
        lg_sum[mine] = acc

    for half in range(HALVES):
        grad_block(half, 0)
        loop(1, side, functools.partial(grad_block, half))

    def gating_back(grad_out, sig, val):
        masked = grad_out * pmask
        return jnp.concatenate([masked * val * sig * (1.0 - sig), masked * sig], axis=-1).astype(
            BF16
        )

    dleft = gating_back(lg_sum[...].reshape(pairs, hidden), left_sig, left_val)
    normalized_gradient = dot_transposed(dleft, pl_ref[...]) + dot_transposed(
        grad_gpre, go_ref[...]
    )

    def add_q(step, running):
        q_copy(0, row ^ step, step).wait_recv()
        return running + q_recv[row ^ step].astype(F32)

    grad_rg = q_send[row].astype(F32)
    if side <= 4:
        for step in range(1, side):
            grad_rg = add_q(step, grad_rg)
    else:
        grad_rg = lax.fori_loop(1, side, add_q, grad_rg)
    dright = gating_back(grad_rg, right_sig, right_val)
    normalized_gradient = normalized_gradient + dot_transposed(dright, pr_ref[...])

    stat_send[0:1, :] = jnp.sum(normalized_gradient, axis=0, keepdims=True)
    stat_send[1:2, :] = jnp.sum(normalized_gradient * xhat, axis=0, keepdims=True)

    def stat_copy(step):
        other = me ^ step
        return pltpu.make_async_remote_copy(
            src_ref=stat_send,
            dst_ref=stat_recv.at[step - 1],
            send_sem=stat_ssem,
            recv_sem=stat_rsem,
            device_id=device(other // side, other % side),
            device_id_type=MESH,
        )

    if peers <= 16:
        for step in range(1, peers):
            stat_copy(step).start()
    else:
        lax.fori_loop(1, peers, lambda step, _: (stat_copy(step).start(), 0)[1], 0)

    pgrad_ref[...] = normalize_backward(
        normalized_gradient * gain_ref[...], xhat, inverse
    ).reshape(rows, cols, chans)
    pgrad_store = pltpu.make_async_copy(pgrad_ref, pgrad_hbm, store_sem.at[1])
    pgrad_store.start()

    def sent(step):
        right_copy(step).wait_send()
        for half in range(HALVES):
            part_copy(half, 0, col ^ step, step).wait_send()
            grad_copy(half, step).wait_send()
        q_copy(0, row ^ step, step).wait_send()

    loop(1, side, sent)
    pltpu.make_async_copy(stat_recv, stat_recv, stat_rsem).wait()
    stats = stat_send[...] + jnp.sum(stat_recv[...], axis=0)
    stats_ref[...] = stats / total
    stats_store = pltpu.make_async_copy(stats_ref, stats_hbm, store_sem.at[2])
    stats_store.start()
    pltpu.make_async_copy(stat_recv, stat_recv, stat_ssem).wait()
    update_store.wait()
    pgrad_store.wait()
    stats_store.wait()


def finish(
    update_in, pgrad_in, stats_in, update_out, pgrad_out, ggrad_out, bgrad_out, update, pgrad, stats, sem
):
    loads = [
        pltpu.make_async_copy(source, target, sem.at[index])
        for index, (source, target) in enumerate(
            ((pgrad_in, pgrad), (update_in, update), (stats_in, stats))
        )
    ]
    stores = [
        pltpu.make_async_copy(source, target, sem.at[index + 3])
        for index, (source, target) in enumerate(
            (
                (pgrad, pgrad_out),
                (update, update_out),
                (stats.at[1:2], ggrad_out),
                (stats.at[0:1], bgrad_out),
            )
        )
    ]
    for load in loads:
        load.start()
    for index in (2, 1, 0):
        loads[index].wait()
        for store in stores[index : 4 if index == 2 else index + 1]:
            store.start()
    for store in stores:
        store.wait()


def on_device(
    side,
    pair,
    res_mask,
    input_norm_gain,
    input_norm_bias,
    proj_left,
    proj_right,
    gate_out,
    mid_gain,
    mid_bias,
    proj_out,
    cotangent,
):
    rows, cols, chans = pair.shape
    hidden = proj_left.shape[1] // 2
    pairs = rows * cols
    blocks = (side, pairs, hidden)
    hbm = pl.BlockSpec(memory_space=pltpu.HBM)
    block = (rows, cols, chans)
    update, pair_gradient, stats = pl.pallas_call(
        functools.partial(kernel, side),
        out_shape=(
            jax.ShapeDtypeStruct((rows, cols, chans), BF16),
            jax.ShapeDtypeStruct((rows, cols, chans), F32),
            jax.ShapeDtypeStruct((2, chans), F32),
        ),
        in_specs=[hbm] * 11,
        out_specs=(hbm,) * 3,
        scratch_shapes=[
            pltpu.VMEM(block, BF16),
            pltpu.VMEM(block, F32),
            pltpu.VMEM((2, chans), F32),
            pltpu.VMEM(block, BF16),
            pltpu.VMEM((1, res_mask.shape[0]), jnp.int32),
            pltpu.VMEM((1, chans), F32),
            pltpu.VMEM((1, chans), F32),
            pltpu.VMEM(proj_left.shape, BF16),
            pltpu.VMEM(proj_right.shape, BF16),
            pltpu.VMEM(gate_out.shape, BF16),
            pltpu.VMEM((1, hidden), F32),
            pltpu.VMEM((1, hidden), F32),
            pltpu.VMEM(proj_out.shape, BF16),
            pltpu.VMEM(block, BF16),
            pltpu.SemaphoreType.DMA((11,)),
            pltpu.SemaphoreType.DMA((3,)),
            pltpu.VMEM(blocks, BF16),
            pltpu.VMEM((side * pairs, hidden), F32),
            pltpu.VMEM((rows, cols, hidden), F32),
            pltpu.VMEM(blocks, BF16),
            pltpu.VMEM(blocks, BF16),
            pltpu.VMEM(blocks, BF16),
            pltpu.VMEM((rows // HALVES, cols, hidden), F32),
            pltpu.VMEM((rows, cols, hidden), F32),
            pltpu.VMEM(blocks, F32),
            pltpu.VMEM(blocks, BF16),
            pltpu.VMEM(blocks, BF16),
            pltpu.VMEM((2, chans), F32),
            pltpu.VMEM((side * side - 1, 2, chans), F32),
        ]
        + [pltpu.SemaphoreType.DMA((side,))] * 2
        + [pltpu.SemaphoreType.DMA((HALVES, side))] * 4
        + [pltpu.SemaphoreType.DMA((side,))] * 2
        + [pltpu.SemaphoreType.DMA] * 2,
        compiler_params=pltpu.CompilerParams(
            collective_id=0, has_side_effects=True, vmem_limit_bytes=VMEM_LIMIT
        ),
        name="triangle",
    )(
        pair,
        res_mask.reshape(1, -1),
        input_norm_gain.reshape(1, -1),
        input_norm_bias.reshape(1, -1),
        proj_left,
        proj_right,
        gate_out,
        mid_gain.reshape(1, -1),
        mid_bias.reshape(1, -1),
        proj_out,
        cotangent,
    )
    update, pair_gradient, gain_gradient, grad_bias = pl.pallas_call(
        finish,
        out_shape=(
            jax.ShapeDtypeStruct(block, BF16),
            jax.ShapeDtypeStruct(block, F32),
            jax.ShapeDtypeStruct((1, chans), F32),
            jax.ShapeDtypeStruct((1, chans), F32),
        ),
        in_specs=[hbm] * 3,
        out_specs=(hbm,) * 4,
        scratch_shapes=[
            pltpu.VMEM(block, BF16),
            pltpu.VMEM(block, F32),
            pltpu.VMEM((2, chans), F32),
            pltpu.SemaphoreType.DMA((7,)),
        ],
        compiler_params=pltpu.CompilerParams(vmem_limit_bytes=VMEM_LIMIT),
        name="finish",
    )(update, pair_gradient, stats)
    return update, pair_gradient, gain_gradient.reshape(-1), grad_bias.reshape(-1)


def solution(mesh):
    blocks = P(("groups", "row"), "col", None)
    return jax.shard_map(
        functools.partial(on_device, mesh.shape["row"]),
        mesh=mesh,
        in_specs=(blocks, P("groups")) + (P(),) * 8 + (blocks,),
        out_specs=(blocks, blocks, P("groups"), P("groups")),
        check_vma=False,
    )
```

```python
import functools

import jax
import jax.numpy as jnp
from jax import lax
from jax.experimental import pallas as pl
from jax.experimental.pallas import tpu as pltpu
from jax.sharding import PartitionSpec as P

MESH = pl.DeviceIdType.MESH
F32 = jnp.float32
BF16 = jnp.bfloat16
VMEM_LIMIT = 62 * 1024 * 1024
HALVES = 2


def normalize(values):
    center = values - jnp.mean(values, axis=-1, keepdims=True)
    inverse = lax.rsqrt(jnp.mean(center * center, axis=-1, keepdims=True) + 1e-05)
    return center * inverse, inverse


def normalize_backward(grad_hat, hatted, inverse):
    first = jnp.mean(grad_hat, axis=-1, keepdims=True)
    second = jnp.mean(grad_hat * hatted, axis=-1, keepdims=True)
    return (grad_hat - first - hatted * second) * inverse


def dot(a, b):
    return jnp.dot(a, b, preferred_element_type=F32)


def dot_transposed(a, b):
    return lax.dot_general(a, b, (((1,), (1,)), ((), ())), preferred_element_type=F32)


def loop(low, high, body):
    if high - low <= 4:
        for step in range(low, high):
            body(step)
    else:
        lax.fori_loop(low, high, lambda step, _: (body(step), 0)[1], 0)


def kernel(
    side,
    pair_hbm,
    mask_hbm,
    gain_hbm,
    bias_hbm,
    pl_hbm,
    pr_hbm,
    go_hbm,
    mgain_hbm,
    mbias_hbm,
    po_hbm,
    cot_hbm,
    update_hbm,
    pgrad_hbm,
    stats_hbm,
    update_ref,
    pgrad_ref,
    stats_ref,
    pair_ref,
    mask_ref,
    gain_ref,
    bias_ref,
    pl_ref,
    pr_ref,
    go_ref,
    mgain_ref,
    mbias_ref,
    po_ref,
    cot_ref,
    load_sem,
    store_sem,
    right_all,
    right32,
    left32,
    part_send,
    part_recv,
    grad_all,
    grad32,
    lg_sum,
    q_sum,
    q_send,
    q_recv,
    stat_send,
    stat_recv,
    right_ssem,
    right_rsem,
    part_ssem,
    part_rsem,
    grad_ssem,
    grad_rsem,
    q_ssem,
    q_rsem,
    stat_ssem,
    stat_rsem,
):
    loads = [
        pltpu.make_async_copy(source, target, load_sem.at[index])
        for index, (source, target) in enumerate(
            (
                (pair_hbm, pair_ref),
                (gain_hbm, gain_ref),
                (bias_hbm, bias_ref),
                (mask_hbm, mask_ref),
                (pr_hbm, pr_ref),
                (pl_hbm, pl_ref),
                (go_hbm, go_ref),
                (cot_hbm, cot_ref),
                (po_hbm, po_ref),
                (mgain_hbm, mgain_ref),
                (mbias_hbm, mbias_ref),
            )
        )
    ]
    for load in loads:
        load.start()

    rows, cols, chans = pair_ref.shape
    pairs = rows * cols
    hidden = pl_ref.shape[1] // 2
    total = mask_ref.shape[1]
    peers = side * side
    row = lax.axis_index("row")
    col = lax.axis_index("col")
    me = row * side + col

    def device(r, c):
        return {"row": r, "col": c}

    barrier = pltpu.get_barrier_semaphore()

    def greet(step):
        other = me ^ step
        pl.semaphore_signal(
            barrier, inc=1, device_id=device(other // side, other % side), device_id_type=MESH
        )

    if peers <= 16:
        for step in range(1, peers):
            greet(step)
    else:
        lax.fori_loop(1, peers, lambda step, _: (greet(step), 0)[1], 0)

    loads[0].wait()
    xhat, inverse = normalize(pair_ref[...].reshape(pairs, chans).astype(F32))
    for load in loads[1:5]:
        load.wait()
    normed = (xhat * gain_ref[...] + bias_ref[...]).astype(BF16)

    spot = lax.broadcasted_iota(jnp.int32, (pairs, total), 0)
    lane = lax.broadcasted_iota(jnp.int32, (pairs, total), 1)
    maskf = mask_ref[...].astype(F32)
    mask_row = jnp.sum(
        jnp.where(lane == row * rows + spot // cols, maskf, 0.0), axis=-1, keepdims=True
    )
    mask_col = jnp.sum(
        jnp.where(lane == col * cols + spot % cols, maskf, 0.0), axis=-1, keepdims=True
    )
    pmask = mask_row * mask_col

    right = dot(normed, pr_ref[...])
    right_sig = jax.nn.sigmoid(right[:, :hidden])
    right_val = right[:, hidden:]
    right_all[row] = (pmask * right_sig * right_val).astype(BF16)

    pl.semaphore_wait(barrier, peers - 1)

    def right_copy(step):
        return pltpu.make_async_remote_copy(
            src_ref=right_all.at[row],
            dst_ref=right_all.at[row],
            send_sem=right_ssem.at[step],
            recv_sem=right_rsem.at[step],
            device_id=device(row ^ step, col),
            device_id_type=MESH,
        )

    right_copy(1).start()
    loop(1, side // 2, lambda half_step: right_copy(2 * half_step).start())

    def right_relay(step):
        return pltpu.make_async_remote_copy(
            src_ref=right_all.at[row ^ step],
            dst_ref=right_all.at[row ^ step],
            send_sem=right_ssem.at[step + 1],
            recv_sem=right_rsem.at[step + 1],
            device_id=device(row ^ 1, col),
            device_id_type=MESH,
        )

    for load in loads[5:]:
        load.wait()
    left = dot(normed, pl_ref[...])
    left_sig = jax.nn.sigmoid(left[:, :hidden])
    left_val = left[:, hidden:]
    left_gated = (pmask * left_sig * left_val).astype(BF16).astype(F32)
    left32[...] = left_gated.reshape(rows, cols, hidden)
    gate = jax.nn.sigmoid(dot(normed, go_ref[...]))

    part = pairs // HALVES
    span = rows // HALVES

    def part_copy(half, slot, c, step):
        place = pl.ds(half * part, part)
        return pltpu.make_async_remote_copy(
            src_ref=part_send.at[slot, place],
            dst_ref=part_recv.at[col, place],
            send_sem=part_ssem.at[half, step],
            recv_sem=part_rsem.at[half, step],
            device_id=device(row, c),
            device_id_type=MESH,
        )

    def take_right(step):
        block = row ^ step
        if not (isinstance(step, int) and step == 0):
            right_copy(step).wait_recv()
            if isinstance(step, int):
                if step % 2 == 0:
                    right_relay(step).start()
            else:

                @pl.when(lax.rem(step, 2) == 0)
                def _():
                    right_relay(step).start()

        base = pl.multiple_of(block * pairs, pairs)
        right32[pl.ds(base, pairs), :] = right_all[block].astype(F32)

    def product_block(half, step):
        block = row ^ step
        base = pl.multiple_of(block * pairs, pairs)
        acc = None
        for k in range(cols):
            term = (
                left32[half * span : (half + 1) * span, k : k + 1, :]
                * right32[pl.ds(base + k, rows, stride=cols), :][None]
            )
            acc = term if acc is None else acc + term
        part_send[block, half * part : (half + 1) * part, :] = acc.reshape(part, hidden).astype(
            BF16
        )

        @pl.when(block != col)
        def _():
            part_copy(half, block, block, col ^ block).start()

    take_right(0)
    for half in range(HALVES):
        product_block(half, 0)
    if side <= 4:
        for step in range(1, side):
            take_right(step)
            for half in range(HALVES):
                product_block(half, step)
    else:

        def take_and_multiply(step):
            take_right(step)
            for half in range(HALVES):
                product_block(half, step)

        loop(1, side, take_and_multiply)

    def grad_copy(half, step):
        place = pl.ds(half * part, part)
        return pltpu.make_async_remote_copy(
            src_ref=grad_all.at[col, place],
            dst_ref=grad_all.at[col, place],
            send_sem=grad_ssem.at[half, step],
            recv_sem=grad_rsem.at[half, step],
            device_id=device(row, col ^ step),
            device_id_type=MESH,
        )

    upstream = cot_ref[...].reshape(pairs, chans).astype(F32)
    grad_value = (upstream * gate).astype(BF16)
    grad_mid = dot_transposed(grad_value, po_ref[...]) * mgain_ref[...]
    values = []

    for half in range(HALVES):
        own = slice(half * part, (half + 1) * part)

        def add_part(step, running):
            part_copy(half, 0, col ^ step, step).wait_recv()
            return running + part_recv[col ^ step, own, :].astype(F32)

        product = part_send[col, own, :].astype(F32)
        if side <= 4:
            for step in range(1, side):
                product = add_part(step, product)
        else:
            product = lax.fori_loop(1, side, add_part, product)
        ohat, oinv = normalize(product)
        grad_product = normalize_backward(grad_mid[own], ohat, oinv)
        grad_all[col, own, :] = grad_product.astype(BF16)
        loop(1, side, lambda step: grad_copy(half, step).start())
        mid = (ohat * mgain_ref[...] + mbias_ref[...]).astype(BF16)
        values.append(dot(mid, po_ref[...]))

    value = jnp.concatenate(values, axis=0)
    update_ref[...] = (gate * value).astype(BF16).reshape(rows, cols, chans)
    update_store = pltpu.make_async_copy(update_ref, update_hbm, store_sem.at[0])
    update_store.start()
    grad_gpre = (upstream * value * gate * (1.0 - gate)).astype(BF16)

    def q_copy(slot, r, sem):
        return pltpu.make_async_remote_copy(
            src_ref=q_send.at[slot],
            dst_ref=q_recv.at[row],
            send_sem=q_ssem.at[sem],
            recv_sem=q_rsem.at[sem],
            device_id=device(r, col),
            device_id_type=MESH,
        )

    lg_sum[...] = jnp.zeros_like(lg_sum)

    def take_grad(half, step):
        own = slice(half * part, (half + 1) * part)
        if not (isinstance(step, int) and step == 0):
            grad_copy(half, step).wait_recv()
        grad32[col ^ step] = grad_all[col ^ step, own, :].astype(F32).reshape(span, cols, hidden)

    def scatter_block(half, step):
        block = col ^ step
        mine = slice(half * span, (half + 1) * span)
        for j in range(cols):
            term = jnp.sum(grad32[block, :, j : j + 1, :] * left32[mine], axis=0)
            where = slice(j * cols, (j + 1) * cols)
            if half > 0:
                term = term + q_sum[block, where, :]
            if half < HALVES - 1:
                q_sum[block, where, :] = term
            else:
                q_send[block, where, :] = term.astype(BF16)

        if half == HALVES - 1:

            @pl.when(block != row)
            def _():
                q_copy(block, block, row ^ block).start()

    def gather_block(half, step):
        block = col ^ step
        mine = slice(half * span, (half + 1) * span)
        acc = lg_sum[mine]
        base = pl.multiple_of(block * pairs, pairs)
        for j in range(cols):
            acc = (
                acc
                + grad32[block, :, j : j + 1, :]
                * right32[pl.ds(base + j * cols, cols), :][None]
            )
        lg_sum[mine] = acc

    for half in range(HALVES):

        def scatter_step(step):
            take_grad(half, step)
            scatter_block(half, step)
            if half < HALVES - 1:
                gather_block(half, step)

        scatter_step(0)
        loop(1, side, scatter_step)
    gather_block(HALVES - 1, 0)
    loop(1, side, functools.partial(gather_block, HALVES - 1))

    def gating_back(grad_out, sig, val):
        masked = grad_out * pmask
        return jnp.concatenate([masked * val * sig * (1.0 - sig), masked * sig], axis=-1).astype(
            BF16
        )

    dleft = gating_back(lg_sum[...].reshape(pairs, hidden), left_sig, left_val)
    normalized_gradient = dot_transposed(dleft, pl_ref[...]) + dot_transposed(
        grad_gpre, go_ref[...]
    )

    def add_q(step, running):
        q_copy(0, row ^ step, step).wait_recv()
        return running + q_recv[row ^ step].astype(F32)

    grad_rg = q_send[row].astype(F32)
    if side <= 4:
        for step in range(1, side):
            grad_rg = add_q(step, grad_rg)
    else:
        grad_rg = lax.fori_loop(1, side, add_q, grad_rg)
    dright = gating_back(grad_rg, right_sig, right_val)
    normalized_gradient = normalized_gradient + dot_transposed(dright, pr_ref[...])

    stat_send[0:1, :] = jnp.sum(normalized_gradient, axis=0, keepdims=True)
    stat_send[1:2, :] = jnp.sum(normalized_gradient * xhat, axis=0, keepdims=True)

    def stat_copy(step):
        other = me ^ step
        return pltpu.make_async_remote_copy(
            src_ref=stat_send,
            dst_ref=stat_recv.at[step - 1],
            send_sem=stat_ssem,
            recv_sem=stat_rsem,
            device_id=device(other // side, other % side),
            device_id_type=MESH,
        )

    if peers <= 16:
        for step in range(1, peers):
            stat_copy(step).start()
    else:
        lax.fori_loop(1, peers, lambda step, _: (stat_copy(step).start(), 0)[1], 0)

    pgrad_ref[...] = normalize_backward(
        normalized_gradient * gain_ref[...], xhat, inverse
    ).reshape(rows, cols, chans)
    pgrad_store = pltpu.make_async_copy(pgrad_ref, pgrad_hbm, store_sem.at[1])
    pgrad_store.start()

    def sent(step):
        right_copy(step).wait_send()
        for half in range(HALVES):
            part_copy(half, 0, col ^ step, step).wait_send()
            grad_copy(half, step).wait_send()
        q_copy(0, row ^ step, step).wait_send()

    loop(1, side, sent)
    pltpu.make_async_copy(stat_recv, stat_recv, stat_rsem).wait()
    stats = stat_send[...] + jnp.sum(stat_recv[...], axis=0)
    stats_ref[...] = stats / total
    stats_store = pltpu.make_async_copy(stats_ref, stats_hbm, store_sem.at[2])
    stats_store.start()
    pltpu.make_async_copy(stat_recv, stat_recv, stat_ssem).wait()
    update_store.wait()
    pgrad_store.wait()
    stats_store.wait()


def finish(
    update_in, pgrad_in, stats_in, update_out, pgrad_out, ggrad_out, bgrad_out, update, pgrad, stats, sem
):
    loads = [
        pltpu.make_async_copy(source, target, sem.at[index])
        for index, (source, target) in enumerate(
            ((pgrad_in, pgrad), (update_in, update), (stats_in, stats))
        )
    ]
    stores = [
        pltpu.make_async_copy(source, target, sem.at[index + 3])
        for index, (source, target) in enumerate(
            (
                (pgrad, pgrad_out),
                (update, update_out),
                (stats.at[1:2], ggrad_out),
                (stats.at[0:1], bgrad_out),
            )
        )
    ]
    for load in loads:
        load.start()
    for index in (2, 1, 0):
        loads[index].wait()
        for store in stores[index : 4 if index == 2 else index + 1]:
            store.start()
    for store in stores:
        store.wait()


def on_device(
    side,
    pair,
    res_mask,
    input_norm_gain,
    input_norm_bias,
    proj_left,
    proj_right,
    gate_out,
    mid_gain,
    mid_bias,
    proj_out,
    cotangent,
):
    rows, cols, chans = pair.shape
    hidden = proj_left.shape[1] // 2
    pairs = rows * cols
    blocks = (side, pairs, hidden)
    hbm = pl.BlockSpec(memory_space=pltpu.HBM)
    block = (rows, cols, chans)
    update, pair_gradient, stats = pl.pallas_call(
        functools.partial(kernel, side),
        out_shape=(
            jax.ShapeDtypeStruct((rows, cols, chans), BF16),
            jax.ShapeDtypeStruct((rows, cols, chans), F32),
            jax.ShapeDtypeStruct((2, chans), F32),
        ),
        in_specs=[hbm] * 11,
        out_specs=(hbm,) * 3,
        scratch_shapes=[
            pltpu.VMEM(block, BF16),
            pltpu.VMEM(block, F32),
            pltpu.VMEM((2, chans), F32),
            pltpu.VMEM(block, BF16),
            pltpu.VMEM((1, res_mask.shape[0]), jnp.int32),
            pltpu.VMEM((1, chans), F32),
            pltpu.VMEM((1, chans), F32),
            pltpu.VMEM(proj_left.shape, BF16),
            pltpu.VMEM(proj_right.shape, BF16),
            pltpu.VMEM(gate_out.shape, BF16),
            pltpu.VMEM((1, hidden), F32),
            pltpu.VMEM((1, hidden), F32),
            pltpu.VMEM(proj_out.shape, BF16),
            pltpu.VMEM(block, BF16),
            pltpu.SemaphoreType.DMA((11,)),
            pltpu.SemaphoreType.DMA((3,)),
            pltpu.VMEM(blocks, BF16),
            pltpu.VMEM((side * pairs, hidden), F32),
            pltpu.VMEM((rows, cols, hidden), F32),
            pltpu.VMEM(blocks, BF16),
            pltpu.VMEM(blocks, BF16),
            pltpu.VMEM(blocks, BF16),
            pltpu.VMEM((side, rows // HALVES, cols, hidden), F32),
            pltpu.VMEM((rows, cols, hidden), F32),
            pltpu.VMEM(blocks, F32),
            pltpu.VMEM(blocks, BF16),
            pltpu.VMEM(blocks, BF16),
            pltpu.VMEM((2, chans), F32),
            pltpu.VMEM((side * side - 1, 2, chans), F32),
        ]
        + [pltpu.SemaphoreType.DMA((side,))] * 2
        + [pltpu.SemaphoreType.DMA((HALVES, side))] * 4
        + [pltpu.SemaphoreType.DMA((side,))] * 2
        + [pltpu.SemaphoreType.DMA] * 2,
        compiler_params=pltpu.CompilerParams(
            collective_id=0, has_side_effects=True, vmem_limit_bytes=VMEM_LIMIT
        ),
        name="triangle",
    )(
        pair,
        res_mask.reshape(1, -1),
        input_norm_gain.reshape(1, -1),
        input_norm_bias.reshape(1, -1),
        proj_left,
        proj_right,
        gate_out,
        mid_gain.reshape(1, -1),
        mid_bias.reshape(1, -1),
        proj_out,
        cotangent,
    )
    update, pair_gradient, gain_gradient, grad_bias = pl.pallas_call(
        finish,
        out_shape=(
            jax.ShapeDtypeStruct(block, BF16),
            jax.ShapeDtypeStruct(block, F32),
            jax.ShapeDtypeStruct((1, chans), F32),
            jax.ShapeDtypeStruct((1, chans), F32),
        ),
        in_specs=[hbm] * 3,
        out_specs=(hbm,) * 4,
        scratch_shapes=[
            pltpu.VMEM(block, BF16),
            pltpu.VMEM(block, F32),
            pltpu.VMEM((2, chans), F32),
            pltpu.SemaphoreType.DMA((7,)),
        ],
        compiler_params=pltpu.CompilerParams(vmem_limit_bytes=VMEM_LIMIT),
        name="finish",
    )(update, pair_gradient, stats)
    return update, pair_gradient, gain_gradient.reshape(-1), grad_bias.reshape(-1)


def solution(mesh):
    blocks = P(("groups", "row"), "col", None)
    return jax.shard_map(
        functools.partial(on_device, mesh.shape["row"]),
        mesh=mesh,
        in_specs=(blocks, P("groups")) + (P(),) * 8 + (blocks,),
        out_specs=(blocks, blocks, P("groups"), P("groups")),
        check_vma=False,
    )
```
